256 devices in a mesh: shot: 16 (over x, z_lo), tm: 16 (over z_hi, y, core).
Axes of the slice: x: 4, y: 4, z: 8 (z_hi: 2, z_lo: 4; z = z_hi * 4 + z_lo), core: 2. Of those that a mesh axis runs over, the one named last changes fastest.
Arguments:
- noisy_gather: float32 [32, 1024, 128], P('shot', 'tm'), may hold values from -6 to 6
- observed: float32 [32, 1024, 128], P(None, 'tm', 'shot')
- missing: int32 [32, 128], P('shot'), may hold values 0 or 1
- noise_level: float32 [32], P('shot'), may hold values from 0.05 to 0.95
- dilations: int32 [2], replicated, may hold values from 1 to 16, as said below
- lift_weight: float32 [3, 64], replicated, may hold values from -4 to 4
- level_weight: float32 [64], replicated, may hold values from -4 to 4
- norm_gain: float32 [2, 64], replicated, may hold values from 0.1 to 1.9
- conv_weight: bfloat16 [2, 9, 64, 256], replicated, may hold values from -0.25 to 0.25
- out_weight: bfloat16 [2, 256, 64], replicated, may hold values from -0.375 to 0.375
- head_weight: float32 [64], replicated, may hold values from -0.75 to 0.75
Outputs:
- predicted_noise: float32 [32, 1024, 128], P('shot', 'tm')
The draws below stay inside these ranges and needn't reach their ends.
Inputs may be any that keep to these rules, and one draw needn't show every extreme that they name: `dilations`: each dilation is 1, 2, 4, 8 or 16, and one of them is 16.
All inputs are finite; a program needn't handle non-finite values. No bound on the sum of `missing` on one device may be relied on, other than what follows from the above.
Results may differ from the reference program's by a relative error of at most 0.0039.
Values may be sent and summed in bfloat16 or wider, within the bound.
A program may use at most 128 MiB of HBM per device.

```python
import jax
import jax.numpy as jnp
from jax import lax

CIN = 64
CHID = 256
R = 128
LAYERS = 2
DMAX = 16
SHOTS = 32
NT = 1024


def draw_observed(key, part):
    key = jax.random.fold_in(key, 1)
    first_key = jax.random.fold_in(key, 0)
    times = jnp.arange(NT, dtype=jnp.float32) / NT
    values = jax.random.normal(first_key, (SHOTS, NT, R), jnp.float32)
    envelope = jnp.exp(-1.5 * times)[None, :, None]
    return values * envelope


def draw_dilations(key, part):
    key = jax.random.fold_in(key, 2)
    first_key, second_key = jax.random.split(key)
    table = jnp.array([1, 2, 4, 8], jnp.int32)
    picks = jax.random.randint(first_key, (LAYERS,), 0, 4)
    others = table[picks]
    spot = jax.random.randint(second_key, (), 0, LAYERS)
    return jnp.where(jnp.arange(LAYERS) == spot, DMAX, others).astype(jnp.int32)


def with_ends(entries, stream_key, smallest, top_value):
    dims = entries.shape
    place = [jax.random.randint(jax.random.fold_in(stream_key, axis), (), 0, dims[axis]) for axis in range(len(dims))]
    entries = entries.at[tuple(place)].set(smallest)
    longest = dims.index(max(dims))
    place[longest] = (place[longest] + 1) % dims[longest]
    return entries.at[tuple(place)].set(top_value)


def shard_levels(stream_key, shape, shards, least, high):
    loudness = 1.0
    for position, parts in shards:
        steps = jax.random.uniform(jax.random.fold_in(jax.random.fold_in(stream_key, 6), position), (parts,), jnp.float32, least / len(shards), high / len(shards))
        loudness = loudness * jnp.repeat(jnp.exp(steps), shape[position] // parts).reshape((-1,) + (1,) * (len(shape) - 1 - position))
    return loudness


def gaussian(key, shape, scale, bound, shards=(), held_as=jnp.bfloat16):
    values = scale * jax.random.normal(key, shape, jnp.float32)
    if shards:
        values = values * shard_levels(key, shape, shards, -0.22, 0.18)
    return jnp.clip(values, -bound, bound).astype(held_as)


def setup_inputs(seed: int = 0) -> dict:
    keys = jax.random.split(jax.random.key(seed), 12)
    return {
        "noisy_gather": gaussian(keys[0], (SHOTS, NT, R), 1.0, 6.0, ((0, 16), (1, 16)), jnp.float32),
        "observed": draw_observed(jax.random.fold_in(keys[11], 71), 0),
        "missing": with_ends((jax.random.randint(keys[2], (SHOTS, R), 0, 10) < 3).astype(jnp.int32), jax.random.fold_in(keys[2], 1), 0, 1),
        "noise_level": jnp.clip(0.05 + 0.9 * jax.random.uniform(keys[3], (SHOTS,), jnp.float32) ** shard_levels(keys[3], (SHOTS,), ((0, 16),), -0.2, 0.2), 0.05, 0.95),
        "dilations": draw_dilations(jax.random.fold_in(keys[11], 71), 0),
        "lift_weight": gaussian(keys[5], (3, CIN), 1.0, 4.0, (), jnp.float32),
        "level_weight": gaussian(keys[6], (CIN,), 1.0, 4.0, (), jnp.float32),
        "norm_gain": jnp.clip(1.0 + 0.18 * jax.random.normal(keys[7], (LAYERS, CIN), jnp.float32), 0.1, 1.9),
        "conv_weight": gaussian(keys[8], (LAYERS, 9, CIN, CHID), (9 * CIN) ** -0.5, 0.25),
        "out_weight": gaussian(keys[9], (LAYERS, CHID, CIN), CHID ** -0.5, 0.375),
        "head_weight": gaussian(keys[10], (CIN,), CIN ** -0.5, 0.75, (), jnp.float32),
    }


def lift_inputs(noisy, condition, present, level, lift_weight, level_weight):
    state = lift_weight[0][None, :, None, None] * noisy[:, None]
    state = state + lift_weight[1][None, :, None, None] * condition[:, None]
    state = state + lift_weight[2][None, :, None, None] * present[:, None, None, :]
    return state + level[:, None, None, None] * level_weight[None, :, None, None]

def normalize(state, gain):
    mean_square = lax.optimization_barrier(jnp.mean(state * state, axis=1, keepdims=True))
    return (state * lax.rsqrt(mean_square + 1e-05) * gain[None, :, None, None]).astype(jnp.bfloat16)

def conv_layer(padded, kernel, dilation):
    widened = jnp.pad(padded, ((0, 0), (0, 0), (0, 0), (DMAX, DMAX)))
    length = padded.shape[2] - 2 * DMAX
    columns = padded.shape[3]
    tap_list = []
    for row_tap in range(3):
        for col_tap in range(3):
            time_start = DMAX + (row_tap - 1) * dilation
            recv_start = DMAX + (col_tap - 1) * dilation
            window = lax.dynamic_slice_in_dim(widened, time_start, length, 2)
            window = lax.dynamic_slice_in_dim(window, recv_start, columns, 3)
            tap_list.append(window)
    stacked = jnp.stack(tap_list, 0).astype(jnp.float32)
    return jnp.einsum('kscyx,kco->soyx', stacked, kernel.astype(jnp.float32))

def reference(noisy_gather, observed, missing, noise_level, dilations, lift_weight, level_weight, norm_gain, conv_weight, out_weight, head_weight):
    present = (1 - missing).astype(jnp.float32)
    masked = observed * present[:, None, :]
    energy = lax.optimization_barrier(jnp.sum(masked * masked, axis=(1, 2)))
    cond_scale = lax.rsqrt(energy / (NT * R) + 1e-05)
    condition = masked * cond_scale[:, None, None]

    def per_shot(items):
        noisy, cond, shot_present, level = items
        state = lift_inputs(noisy[None], cond[None], shot_present[None], level[None], lift_weight, level_weight)
        for layer in range(LAYERS):
            normed = normalize(state, norm_gain[layer])
            padded = jnp.pad(normed, ((0, 0), (0, 0), (DMAX, DMAX), (0, 0)))
            summed = conv_layer(padded, conv_weight[layer], dilations[layer])
            activated = jax.nn.gelu(summed).astype(jnp.bfloat16)
            state = state + jnp.einsum('soyx,oc->scyx', activated.astype(jnp.float32), out_weight[layer].astype(jnp.float32))
        return jnp.einsum('scyx,c->syx', state, head_weight, precision=lax.Precision.HIGHEST)[0]
    return lax.map(per_shot, (noisy_gather, condition, present, noise_level))
```

```python
import jax
import jax.numpy as jnp
from jax import lax
from jax.experimental import pallas as pl
from jax.experimental.pallas import tpu as pltpu
from jax.sharding import PartitionSpec as P

MESH = pl.DeviceIdType.MESH
DMAX = 16
HALO = 2 * DMAX
TANH_SCALE = 0.7978845608028654
TANH_CUBE = 0.044715
UNROLL = 4


def comm_kernel(
    shots, spans, obs, noisy, missing, obs_ext, noisy_ext, energy,
    landed, sums, sent, shot_send, shot_recv, halo_send, halo_recv, sum_send, sum_recv,
):
    me_shot = lax.axis_index("shot")
    me_tm = lax.axis_index("tm")
    steps = noisy.shape[1]
    barrier = pltpu.get_barrier_semaphore()
    for step in range(1, shots):
        pl.semaphore_signal(
            barrier, inc=1, device_id={"shot": lax.rem(me_shot + step, shots)}, device_id_type=MESH
        )
    for step in range(1, spans):
        pl.semaphore_signal(
            barrier, inc=1, device_id={"tm": lax.rem(me_tm + step, spans)}, device_id_type=MESH
        )
    pl.semaphore_wait(barrier, shots + spans - 2)

    right = {"tm": lax.rem(me_tm + 1, spans)}
    left = {"tm": lax.rem(me_tm + spans - 1, spans)}

    def halo(source, first, target, slot):
        up = pltpu.make_async_remote_copy(
            src_ref=source.at[:, pl.ds(first + steps - HALO, HALO), :],
            dst_ref=target.at[:, pl.ds(0, HALO), :],
            send_sem=halo_send.at[slot], recv_sem=halo_recv.at[slot],
            device_id=right, device_id_type=MESH,
        )
        down = pltpu.make_async_remote_copy(
            src_ref=source.at[:, pl.ds(first, HALO), :],
            dst_ref=target.at[:, pl.ds(HALO + steps, HALO), :],
            send_sem=halo_send.at[slot + 1], recv_sem=halo_recv.at[slot + 1],
            device_id=left, device_id_type=MESH,
        )
        up.start()
        down.start()
        return [up, down]

    exchange = []
    for step in range(1, shots):
        other = lax.rem(me_shot + step, shots)
        copy = pltpu.make_async_remote_copy(
            src_ref=obs.at[pl.ds(2 * other, 2)], dst_ref=landed.at[me_shot],
            send_sem=shot_send.at[step], recv_sem=shot_recv.at[step],
            device_id={"shot": other}, device_id_type=MESH,
        )
        copy.start()
        exchange.append(copy)
    halos = halo(noisy, 0, noisy_ext, 0)
    landed[me_shot] = obs[pl.ds(2 * me_shot, 2)]
    noisy_ext[:, HALO : HALO + steps, :] = noisy[...]
    for copy in exchange:
        copy.wait_recv()
    rows = jnp.stack([landed[:, s].reshape(8 * shots, steps).T for s in range(2)])
    obs_ext[:, HALO : HALO + steps, :] = rows
    halos += halo(obs_ext, HALO, obs_ext, 2)
    masked = rows * (1 - missing[...]).astype(jnp.float32)[:, None, :]
    sent[...] = jnp.sum(masked * masked, axis=1)
    sharing = []
    for step in range(1, spans):
        other = lax.rem(me_tm + step, spans)
        copy = pltpu.make_async_remote_copy(
            src_ref=sent, dst_ref=sums.at[me_tm],
            send_sem=sum_send.at[step], recv_sem=sum_recv.at[step],
            device_id={"tm": other}, device_id_type=MESH,
        )
        copy.start()
        sharing.append(copy)
    sums[me_tm] = sent[...]
    for copy in sharing:
        copy.wait_recv()
    total = jnp.sum(sums[...], axis=0)
    energy[...] = jnp.broadcast_to(jnp.sum(total, axis=1, keepdims=True), energy.shape)
    for copy in exchange + sharing:
        copy.wait_send()
    for copy in halos:
        copy.wait()


def exchange_inputs(shots, spans, obs, noisy, missing):
    steps = noisy.shape[1]
    vm = pl.BlockSpec(memory_space=pltpu.VMEM)
    ext = jax.ShapeDtypeStruct((2, steps + 2 * HALO, 8 * shots), jnp.float32)
    dma = pltpu.SemaphoreType.DMA
    return pl.pallas_call(
        lambda *refs: comm_kernel(shots, spans, *refs),
        out_shape=(ext, ext, jax.ShapeDtypeStruct((2, 128), jnp.float32)),
        in_specs=[vm] * 3,
        out_specs=(vm,) * 3,
        scratch_shapes=[
            pltpu.VMEM((shots, 2, 8, steps), jnp.float32),
            pltpu.VMEM((spans, 2, 128), jnp.float32),
            pltpu.VMEM((2, 128), jnp.float32),
            dma((shots,)), dma((shots,)), dma((4,)), dma((4,)), dma((spans,)), dma((spans,)),
        ],
        compiler_params=pltpu.CompilerParams(
            collective_id=0, has_side_effects=True, vmem_limit_bytes=32 * 2**20
        ),
        name="exchange",
    )(obs, noisy, missing)


def gelu_of_half(h):
    u = h * (2 * TANH_SCALE + (8 * TANH_SCALE * TANH_CUBE) * (h * h))
    return (h + h * jnp.tanh(u)).astype(jnp.bfloat16)


def mm(a, b):
    return jnp.dot(a, b, preferred_element_type=jnp.float32)


def column(row):
    return jnp.broadcast_to(jnp.broadcast_to(row, (8, row.shape[1])).T[:, :1], (row.shape[1], 128))


def compute_kernel(
    spans, dil, level, energy, noisy, obs, missing, lift, levw, gain, cw, ow, head, out,
    x1, x2, state, wt, owt, lw,
):
    f32, bf16 = jnp.float32, jnp.bfloat16
    steps = out.shape[1]
    total_time = spans * steps
    d1, d2 = dil[0], dil[1]
    first = lax.axis_index("tm") * steps - HALO

    for l in range(2):
        parts = [[], [], [], []]
        for j in range(3):
            w0, w1, w2 = [cw[l, 3 * i + j].astype(f32) * 0.5 for i in range(3)]
            outer = (w0 + w2) * 0.5
            parts[0].append(w0)
            parts[1].append(outer + w1 * 0.5)
            parts[2].append(outer - w1 * 0.5)
            parts[3].append(w2)
        for k in range(4):
            wt[l, k] = jnp.concatenate(parts[k], 0).T.astype(bf16)
    owt[...] = ow[0]
    head_row = head[...]
    last = lax.dot_general(
        head_row, ow[1].astype(f32), (((1,), (0,)), ((), ())), precision=lax.Precision.HIGHEST
    )
    last_high = last.astype(bf16)
    last_low = (last - last_high.astype(f32)).astype(bf16)
    last_rows = jnp.concatenate([last_high, last_low, jnp.zeros((14, 256), bf16)], 0)
    lane = lax.broadcasted_iota(jnp.int32, (64, 128), 1)

    lw[0] = column(lift[0:1, :])
    lw[1] = column(lift[1:2, :])
    scales = []
    for s in range(2):
        present = (1 - missing[s : s + 1, :]).astype(f32)
        lw[2 + s] = column(lift[2:3, :]) * present + level[s] * column(levw[...])
        scales.append(present * lax.rsqrt(energy[s : s + 1, :] / (total_time * 128) + 1e-5))
    lw[4] = column(gain[0:1, :])
    lw[5] = column(gain[1:2, :])
    lw[6] = column(head_row)

    def put(ref, row, halves, d):
        ref[row, 64:128, :] = jnp.concatenate(halves, 1).astype(bf16)
        low = [jnp.where(lane >= d, pltpu.roll(a, d, 1), 0.0) for a in halves]
        ref[row, 0:64, :] = jnp.concatenate(low, 1).astype(bf16)
        high = [jnp.where(lane < 128 - d, pltpu.roll(a, 128 - d, 1), 0.0) for a in halves]
        ref[row, 128:192, :] = jnp.concatenate(high, 1).astype(bf16)

    def norm(a, g, row):
        time = row + first
        inside = jnp.where(jnp.logical_and(time >= 0, time < total_time), 1.0, 0.0).astype(f32)
        mean_square = jnp.sum(a * a, axis=0, keepdims=True) * (1.0 / 64)
        return a * (lax.rsqrt(mean_square + 1e-5) * inside) * g

    def lift_row(row):
        normed = []
        for s in range(2):
            a = lw[0] * noisy[s, pl.ds(row, 1), :]
            a = a + lw[1] * (obs[s, pl.ds(row, 1), :] * scales[s]) + lw[2 + s]
            state[row, :, s * 128 : (s + 1) * 128] = a
            normed.append(norm(a, lw[4], row))
        put(x1, row, normed, d1)

    def unrolled(count, body, by):
        def several(q, carry):
            for u in range(by):
                body(q * by + u)
            return carry

        lax.fori_loop(0, (count + by - 1) // by, several, 0)

    unrolled(steps + 2 * (d1 + d2), lambda i: lift_row(HALO - d1 - d2 + i), 4)

    def conv_pair(l, ref, r, d, then):
        a0, a1, a2, a3 = ref[r - d], ref[r], ref[r + d], ref[r + 2 * d]
        m1 = mm(wt[l, 1], a1 + a2)
        m2 = mm(wt[l, 2], a2 - a1)
        m0 = mm(wt[l, 0], a0 - a2)
        m3 = mm(wt[l, 3], a1 - a3)
        then(0, gelu_of_half(m0 + (m1 + m2)))
        then(1, gelu_of_half((m1 - m2) - m3))

    def pair_row(p, d):
        block = p // d
        return block * (2 * d) + (p - block * d)

    rows = steps + 2 * d2
    whole = rows // (2 * d1)
    pairs = whole * d1 + jnp.minimum(rows - whole * 2 * d1, d1)

    def first_pair(p):
        r0 = pair_row(p, d1) + HALO - d2

        def then(e, act):
            r = r0 + e * d1
            updated = state[r] + mm(owt[...], act)
            state[r] = updated
            put(x2, r - DMAX, [norm(updated[:, s * 128 : (s + 1) * 128], lw[5], r) for s in range(2)], d2)

        conv_pair(0, x1, r0, d1, then)

    unrolled(pairs, first_pair, UNROLL)

    def second_pair(p):
        r0 = pair_row(p, d2)

        def then(e, act):
            r = r0 + e * d2
            y = mm(last_rows, act)
            y = y[0:1, :] + y[1:2, :]
            for s in range(2):
                lanes = slice(s * 128, (s + 1) * 128)
                h = jnp.sum(state[r + HALO, :, lanes] * lw[6], axis=0, keepdims=True)
                out[s, pl.ds(r, 1), :] = h + y[:, lanes]

        conv_pair(1, x2, r0 + DMAX, d2, then)

    unrolled(steps // 2, second_pair, UNROLL)


def denoise(spans, dil, level, energy, noisy, obs, missing, lift, levw, gain, cw, ow, head):
    steps = noisy.shape[1] - 2 * HALO
    sm = pl.BlockSpec(memory_space=pltpu.SMEM)
    vm = pl.BlockSpec(memory_space=pltpu.VMEM)
    return pl.pallas_call(
        lambda *refs: compute_kernel(spans, *refs),
        out_shape=jax.ShapeDtypeStruct((2, steps, 128), jnp.float32),
        in_specs=[sm, sm] + [vm] * 10,
        out_specs=vm,
        scratch_shapes=[
            pltpu.VMEM((160, 192, 256), jnp.bfloat16),
            pltpu.VMEM((128, 192, 256), jnp.bfloat16),
            pltpu.VMEM((160, 64, 256), jnp.float32),
            pltpu.VMEM((2, 4, 256, 192), jnp.bfloat16),
            pltpu.VMEM((64, 256), jnp.bfloat16),
            pltpu.VMEM((7, 64, 128), jnp.float32),
        ],
        compiler_params=pltpu.CompilerParams(vmem_limit_bytes=50 * 2**20),
        name="denoise",
    )(dil, level, energy, noisy, obs, missing, lift, levw, gain, cw, ow, head)


def solution(mesh):
    shots, spans = mesh.shape["shot"], mesh.shape["tm"]

    def per_device(
        noisy_gather, observed, missing, noise_level, dilations, lift_weight, level_weight,
        norm_gain, conv_weight, out_weight, head_weight,
    ):
        obs_ext, noisy_ext, energy = exchange_inputs(shots, spans, jnp.swapaxes(observed, 1, 2), noisy_gather, missing)
        return denoise(
            spans, dilations, noise_level, energy, noisy_ext, obs_ext, missing, lift_weight,
            level_weight[None, :], norm_gain, conv_weight, jnp.swapaxes(out_weight, 1, 2), head_weight[None, :],
        )

    return jax.shard_map(
        per_device,
        mesh=mesh,
        in_specs=(
            P("shot", "tm", None), P(None, "tm", "shot"), P("shot", None), P("shot"),
            P(), P(), P(), P(), P(), P(), P(),
        ),
        out_specs=P("shot", "tm", None),
        check_vma=False,
    )
```

```python
import jax
import jax.numpy as jnp
from jax import lax
from jax.experimental import pallas as pl
from jax.experimental.pallas import tpu as pltpu
from jax.sharding import PartitionSpec as P

MESH = pl.DeviceIdType.MESH
DMAX = 16
HALO = 2 * DMAX
TANH_SCALE = 0.7978845608028654
TANH_CUBE = 0.044715
UNROLL = 8
f32, bf16 = jnp.float32, jnp.bfloat16


def column(row):
    return jnp.broadcast_to(jnp.broadcast_to(row, (8, row.shape[1])).T[:, :1], (row.shape[1], 128))


def exchange_kernel(
    shots, spans,
    obs, noisy, missing, level, dil, lift, levw, gain, cw, ow, head,
    masked_ext, noisy_ext, scale, cols, shot_base, wt, projection, last, dil_out,
    landed, sums, sent, miss, level_v, lift_v, levw_v, gain_v, cw_v, ow_v, head_v,
    local_sem, shot_send, shot_recv, halo_send, halo_recv, sum_send, sum_recv,
):
    me_shot = lax.axis_index("shot")
    me_tm = lax.axis_index("tm")
    steps = noisy.shape[1]
    barrier = pltpu.get_barrier_semaphore()
    for step in range(1, shots):
        pl.semaphore_signal(
            barrier, inc=1, device_id={"shot": lax.rem(me_shot + step, shots)}, device_id_type=MESH
        )
    for step in range(1, spans):
        pl.semaphore_signal(
            barrier, inc=1, device_id={"tm": lax.rem(me_tm + step, spans)}, device_id_type=MESH
        )
    pairs = [
        (cw, cw_v), (ow, ow_v), (lift, lift_v), (levw, levw_v), (gain, gain_v), (head, head_v),
        (level, level_v), (dil, dil_out), (missing, miss),
        (noisy, noisy_ext.at[:, pl.ds(HALO, steps), :]),
        (obs.at[pl.ds(2 * me_shot, 2)], landed.at[me_shot]),
    ]
    local = [pltpu.make_async_copy(a, b, local_sem.at[i]) for i, (a, b) in enumerate(pairs)]
    for copy in local:
        copy.start()
    pl.semaphore_wait(barrier, shots + spans - 2)

    right = {"tm": lax.rem(me_tm + 1, spans)}
    left = {"tm": lax.rem(me_tm + spans - 1, spans)}

    def halo(source, first, target, slot):
        up = pltpu.make_async_remote_copy(
            src_ref=source.at[:, pl.ds(first + steps - HALO, HALO), :],
            dst_ref=target.at[:, pl.ds(0, HALO), :],
            send_sem=halo_send.at[slot], recv_sem=halo_recv.at[slot],
            device_id=right, device_id_type=MESH,
        )
        down = pltpu.make_async_remote_copy(
            src_ref=source.at[:, pl.ds(first, HALO), :],
            dst_ref=target.at[:, pl.ds(HALO + steps, HALO), :],
            send_sem=halo_send.at[slot + 1], recv_sem=halo_recv.at[slot + 1],
            device_id=left, device_id_type=MESH,
        )
        up.start()
        down.start()
        return [up, down]

    exchange = []
    for step in range(1, shots):
        other = lax.rem(me_shot + step, shots)
        copy = pltpu.make_async_remote_copy(
            src_ref=obs.at[pl.ds(2 * other, 2)], dst_ref=landed.at[me_shot],
            send_sem=shot_send.at[step], recv_sem=shot_recv.at[step],
            device_id={"shot": other}, device_id_type=MESH,
        )
        copy.start()
        exchange.append(copy)
    halos = halo(noisy, 0, noisy_ext, 0)
    for copy in local:
        copy.wait()

    taps = cw.shape[1]
    for l in range(2):
        for k in range(0, taps, 2):
            count = min(2, taps - k)
            block = jnp.concatenate([cw_v[l, k + i] for i in range(count)], 0).astype(f32) * 0.5
            wt[l, :, k * 64 : (k + count) * 64] = block.T.astype(bf16)
    projection[...] = ow_v[0]
    folded = lax.dot_general(
        head_v[...], ow_v[1].astype(f32), (((1,), (0,)), ((), ())), precision=lax.Precision.HIGHEST
    )
    high = folded.astype(bf16)
    low = (folded - high.astype(f32)).astype(bf16)
    last[...] = jnp.concatenate([high, low, jnp.zeros((14, 256), bf16)], 0)
    cols[0] = column(lift_v[0:1, :])
    cols[1] = column(lift_v[1:2, :])
    cols[2] = column(gain_v[0:1, :])
    cols[3] = column(gain_v[1:2, :])
    cols[4] = column(head_v[...])
    present = (1 - miss[...]).astype(f32)
    for s in range(2):
        noise = jnp.broadcast_to(level_v[0:1, s : s + 1], (64, 128))
        shot_base[s] = column(lift_v[2:3, :]) * present[s : s + 1, :] + noise * column(levw_v[...])

    for copy in exchange:
        copy.wait_recv()
    masked = [landed[:, s].reshape(8 * shots, steps).T * present[s : s + 1, :] for s in range(2)]
    for s in range(2):
        sent[s : s + 1, :] = jnp.sum(masked[s] * masked[s], axis=0, keepdims=True)
    sharing = []
    for step in range(1, spans):
        other = lax.rem(me_tm + step, spans)
        copy = pltpu.make_async_remote_copy(
            src_ref=sent, dst_ref=sums.at[me_tm],
            send_sem=sum_send.at[step], recv_sem=sum_recv.at[step],
            device_id={"tm": other}, device_id_type=MESH,
        )
        copy.start()
        sharing.append(copy)
    for s in range(2):
        masked_ext[s, HALO : HALO + steps, :] = masked[s]
    halos += halo(masked_ext, HALO, masked_ext, 2)
    sums[me_tm] = sent[...]
    for copy in exchange:
        copy.wait_send()
    for copy in sharing:
        copy.wait_recv()
    total = jnp.sum(jnp.sum(sums[...], axis=0), axis=1, keepdims=True)
    total = jnp.broadcast_to(total, scale.shape)
    scale[...] = lax.rsqrt(total / (spans * steps * 8 * shots) + 1e-5)
    for copy in sharing:
        copy.wait_send()
    for copy in halos:
        copy.wait()


def exchange_inputs(shots, spans, *args):
    obs, noisy = args[:2]
    steps = noisy.shape[1]
    shape = jax.ShapeDtypeStruct
    ext = shape((2, steps + 2 * HALO, 8 * shots), f32)
    outs = (
        ext, ext, shape((2, 128), f32), shape((5, 64, 128), f32), shape((2, 64, 128), f32),
        shape((2, 256, 576), bf16), shape((64, 256), bf16), shape((16, 256), bf16),
        shape((1, 2), jnp.int32),
    )
    dma = pltpu.SemaphoreType.DMA
    return pl.pallas_call(
        lambda *refs: exchange_kernel(shots, spans, *refs),
        out_shape=outs,
        in_specs=[pl.BlockSpec(memory_space=pltpu.HBM)] * len(args),
        out_specs=(pl.BlockSpec(memory_space=pltpu.VMEM),) * len(outs),
        scratch_shapes=[
            pltpu.VMEM((shots, 2, 8, steps), f32),
            pltpu.VMEM((spans, 2, 128), f32),
            pltpu.VMEM((2, 128), f32),
        ] + [pltpu.VMEM(a.shape, a.dtype) for i, a in enumerate(args) if i in (2, 3, 5, 6, 7, 8, 9, 10)] + [
            dma((11,)), dma((shots,)), dma((shots,)), dma((4,)), dma((4,)), dma((spans,)), dma((spans,)),
        ],
        compiler_params=pltpu.CompilerParams(
            collective_id=0, has_side_effects=True, vmem_limit_bytes=24 * 2**20
        ),
        name="exchange",
    )(*args)


def gelu_of_half(h):
    u = h * (2 * TANH_SCALE + (8 * TANH_SCALE * TANH_CUBE) * (h * h))
    return (h + h * jnp.tanh(u)).astype(bf16)


def mm(a, b):
    return jnp.dot(a, b, preferred_element_type=f32)


def denoise_kernel(
    spans, masked, noisy, scale, cols, shot_base, wt, projection, last, dil, out, x1, x2, state, *sums
):
    steps = out.shape[1]
    total_time = spans * steps
    by = len(sums)
    d1, d2 = dil[0, 0], dil[0, 1]
    first = lax.axis_index("tm") * steps - HALO
    lane = lax.broadcasted_iota(jnp.int32, (64, 128), 1)
    zeros = jnp.zeros((64, 128), bf16)

    def put(ref, row, halves, d):
        halves = [a.astype(bf16) for a in halves]
        ref[row, 64:128, :] = jnp.concatenate(halves, 1)
        low = [jnp.where(lane >= d, pltpu.roll(a, d, 1), zeros) for a in halves]
        ref[row, 0:64, :] = jnp.concatenate(low, 1)
        high = [jnp.where(lane < 128 - d, pltpu.roll(a, 128 - d, 1), zeros) for a in halves]
        ref[row, 128:192, :] = jnp.concatenate(high, 1)

    def norm(a, g, row):
        time = row + first
        inside = jnp.where(jnp.logical_and(time >= 0, time < total_time), 1.0, 0.0).astype(f32)
        mean_square = jnp.sum(a * a, axis=0, keepdims=True) * (1.0 / 64)
        return a * (lax.rsqrt(mean_square + 1e-5) * inside) * g

    def lift_row(row):
        source = jnp.minimum(row, noisy.shape[1] - 1)
        normed = []
        for s in range(2):
            a = cols[0] * noisy[s, pl.ds(source, 1), :]
            a = a + cols[1] * (masked[s, pl.ds(source, 1), :] * scale[s : s + 1, :]) + shot_base[s]
            state[row, :, s * 128 : (s + 1) * 128] = a
            normed.append(norm(a, cols[2], row))
        put(x1, row, normed, d1)

    def conv(l, ref, r, d):
        return mm(wt[l], jnp.concatenate([ref[r - d], ref[r], ref[r + d]], 0))

    start = HALO - d2
    trips = (steps + 2 * d2 + by - 1) // by
    ahead = start - d1

    def lifts(q, carry):
        for u in range(by):
            lift_row(ahead + q * by + u)
        return carry

    before = (2 * d1 + by + by - 1) // by
    lax.fori_loop(0, before, lifts, 0)
    lifted = ahead + before * by
    for u in range(by):
        sums[u][...] = conv(0, x1, start + u, d1)
    for u in range(by):
        lift_row(lifted + u)
    lifted = lifted + by

    def first_end(r, act):
        updated = state[r] + mm(projection[...], act)
        state[r] = updated
        put(x2, r - DMAX, [norm(updated[:, s * 128 : (s + 1) * 128], cols[3], r) for s in range(2)], d2)

    def second_end(r, act):
        y = mm(last[...], act)
        y = y[0:1, :] + y[1:2, :]
        for s in range(2):
            lanes = slice(s * 128, (s + 1) * 128)
            h = jnp.sum(state[r + HALO, :, lanes] * cols[4], axis=0, keepdims=True)
            out[s, pl.ds(r, 1), :] = h + y[:, lanes]

    def first_block(q, carry):
        r = start + q * by
        for u in range(by):
            act = gelu_of_half(sums[u][...])
            sums[u][...] = conv(0, x1, r + by + u, d1)
            first_end(r + u, act)
        for u in range(by):
            lift_row(lifted + q * by + u)
        return carry

    lax.fori_loop(0, trips - 1, first_block, 0)
    r = start + (trips - 1) * by
    for u in range(by):
        act = gelu_of_half(sums[u][...])
        sums[u][...] = conv(1, x2, DMAX + u, d2)
        first_end(r + u, act)

    def second_block(q, carry):
        r = q * by
        for u in range(by):
            act = gelu_of_half(sums[u][...])
            sums[u][...] = conv(1, x2, DMAX + r + by + u, d2)
            second_end(r + u, act)
        return carry

    lax.fori_loop(0, steps // by - 1, second_block, 0)
    for u in range(by):
        second_end(steps - by + u, gelu_of_half(sums[u][...]))


def denoise(spans, *args):
    steps = args[0].shape[1] - 2 * HALO
    vm = pl.BlockSpec(memory_space=pltpu.VMEM)
    return pl.pallas_call(
        lambda *refs: denoise_kernel(spans, *refs),
        out_shape=jax.ShapeDtypeStruct((2, steps, 128), f32),
        in_specs=[vm] * len(args),
        out_specs=vm,
        scratch_shapes=[
            pltpu.VMEM((176, 192, 256), bf16),
            pltpu.VMEM((136, 192, 256), bf16),
            pltpu.VMEM((176, 64, 256), f32),
        ] + [pltpu.VMEM((256, 256), f32)] * UNROLL,
        compiler_params=pltpu.CompilerParams(vmem_limit_bytes=48 * 2**20),
        name="denoise",
    )(*args)


def solution(mesh):
    shots, spans = mesh.shape["shot"], mesh.shape["tm"]

    def per_device(
        noisy_gather, observed, missing, noise_level, dilations, lift_weight, level_weight,
        norm_gain, conv_weight, out_weight, head_weight,
    ):
        shared = exchange_inputs(
            shots, spans, jnp.swapaxes(observed, 1, 2), noisy_gather, missing, noise_level[None, :],
            dilations[None, :], lift_weight, level_weight[None, :], norm_gain, conv_weight,
            jnp.swapaxes(out_weight, 1, 2), head_weight[None, :],
        )
        return denoise(spans, *shared)

    return jax.shard_map(
        per_device,
        mesh=mesh,
        in_specs=(
            P("shot", "tm", None), P(None, "tm", "shot"), P("shot", None), P("shot"),
            P(), P(), P(), P(), P(), P(), P(),
        ),
        out_specs=P("shot", "tm", None),
        check_vma=False,
    )
```

```python
import jax
import jax.numpy as jnp
from jax import lax
from jax.experimental import pallas as pl
from jax.experimental.pallas import tpu as pltpu
from jax.sharding import PartitionSpec as P

MESH = pl.DeviceIdType.MESH
DMAX = 16
HALO = 2 * DMAX
TANH_SCALE = 0.7978845608028654
TANH_CUBE = 0.044715
UNROLL = 8
f32, bf16 = jnp.float32, jnp.bfloat16


def column(row):
    return jnp.broadcast_to(jnp.broadcast_to(row, (8, row.shape[1])).T[:, :1], (row.shape[1], 128))


def exchange_kernel(
    shots, spans,
    obs, noisy, missing, level, lift, levw, gain, cw, ow, head,
    masked_ext, noisy_ext, sums, cols_out, shot_base_out, wt_out, last_out,
    landed, sent, masked, cols, shot_base, wt, last, miss, level_v, lift_v, levw_v, gain_v, cw_v, ow_v, head_v,
    local_sem, out_sem, shot_send, shot_recv, halo_send, halo_recv, sum_send, sum_recv,
):
    me_shot = lax.axis_index("shot")
    me_tm = lax.axis_index("tm")
    steps = noisy.shape[1]
    barrier = pltpu.get_barrier_semaphore()
    for step in range(1, shots):
        pl.semaphore_signal(
            barrier, inc=1, device_id={"shot": lax.rem(me_shot + step, shots)}, device_id_type=MESH
        )
    for step in range(1, spans):
        pl.semaphore_signal(
            barrier, inc=1, device_id={"tm": lax.rem(me_tm + step, spans)}, device_id_type=MESH
        )
    pairs = [
        (cw, cw_v), (ow, ow_v), (lift, lift_v), (levw, levw_v), (gain, gain_v), (head, head_v),
        (level, level_v), (missing, miss),
        (noisy, noisy_ext.at[:, pl.ds(HALO, steps), :]),
        (obs.at[pl.ds(2 * me_shot, 2)], landed.at[me_shot]),
    ]
    local = [pltpu.make_async_copy(a, b, local_sem.at[i]) for i, (a, b) in enumerate(pairs)]
    for copy in local:
        copy.start()
    pl.semaphore_wait(barrier, shots + spans - 2)

    right = {"tm": lax.rem(me_tm + 1, spans)}
    left = {"tm": lax.rem(me_tm + spans - 1, spans)}

    def halo(source, first, target, slot):
        up = pltpu.make_async_remote_copy(
            src_ref=source.at[:, pl.ds(first + steps - HALO, HALO), :],
            dst_ref=target.at[:, pl.ds(0, HALO), :],
            send_sem=halo_send.at[slot], recv_sem=halo_recv.at[slot],
            device_id=right, device_id_type=MESH,
        )
        down = pltpu.make_async_remote_copy(
            src_ref=source.at[:, pl.ds(first, HALO), :],
            dst_ref=target.at[:, pl.ds(HALO + steps, HALO), :],
            send_sem=halo_send.at[slot + 1], recv_sem=halo_recv.at[slot + 1],
            device_id=left, device_id_type=MESH,
        )
        up.start()
        down.start()
        return [up, down]

    exchange = []
    for step in range(1, shots):
        other = lax.rem(me_shot + step, shots)
        copy = pltpu.make_async_remote_copy(
            src_ref=obs.at[pl.ds(2 * other, 2)], dst_ref=landed.at[me_shot],
            send_sem=shot_send.at[step], recv_sem=shot_recv.at[step],
            device_id={"shot": other}, device_id_type=MESH,
        )
        copy.start()
        exchange.append(copy)
    halos = halo(noisy, 0, noisy_ext, 0)
    for copy in local:
        copy.wait()

    taps = cw.shape[1]
    for l in range(2):
        for k in range(0, taps, 2):
            count = min(2, taps - k)
            block = jnp.concatenate([cw_v[l, k + i] for i in range(count)], 0).astype(f32) * 0.5
            wt[l, :, k * 64 : (k + count) * 64] = block.T.astype(bf16)
    folded = lax.dot_general(
        head_v[...], ow_v[1].astype(f32), (((1,), (0,)), ((), ())), precision=lax.Precision.HIGHEST
    )
    high = folded.astype(bf16)
    low = (folded - high.astype(f32)).astype(bf16)
    last[...] = jnp.concatenate([high, low, jnp.zeros((14, 256), bf16)], 0)
    cols[0] = column(lift_v[0:1, :])
    cols[1] = column(lift_v[1:2, :])
    cols[2] = column(gain_v[0:1, :])
    cols[3] = column(gain_v[1:2, :])
    cols[4] = column(head_v[...])
    present = (1 - miss[...]).astype(f32)
    for s in range(2):
        noise = jnp.broadcast_to(level_v[0:1, s : s + 1], (64, 128))
        shot_base[s] = column(lift_v[2:3, :]) * present[s : s + 1, :] + noise * column(levw_v[...])

    results = [
        pltpu.make_async_copy(a, b, out_sem.at[i])
        for i, (a, b) in enumerate([(cols, cols_out), (shot_base, shot_base_out), (wt, wt_out), (last, last_out)])
    ]
    for copy in results:
        copy.start()

    for copy in exchange:
        copy.wait_recv()
    for s in range(2):
        rows = landed[:, s].reshape(8 * shots, steps).T * present[s : s + 1, :]
        masked[s] = rows
        sent[s : s + 1, :] = jnp.sum(rows * rows, axis=0, keepdims=True)
    sharing = []
    for step in range(1, spans):
        other = lax.rem(me_tm + step, spans)
        copy = pltpu.make_async_remote_copy(
            src_ref=sent, dst_ref=sums.at[me_tm],
            send_sem=sum_send.at[step], recv_sem=sum_recv.at[step],
            device_id={"tm": other}, device_id_type=MESH,
        )
        copy.start()
        sharing.append(copy)
    halos += halo(masked, 0, masked_ext, 2)
    mine = [
        pltpu.make_async_copy(sent, sums.at[me_tm], out_sem.at[4]),
        pltpu.make_async_copy(masked, masked_ext.at[:, pl.ds(HALO, steps), :], out_sem.at[5]),
    ]
    for copy in mine:
        copy.start()
    for copy in exchange:
        copy.wait_send()
    for copy in results + mine:
        copy.wait()
    for copy in sharing + halos:
        copy.wait()


def exchange_inputs(shots, spans, *args):
    obs, noisy = args[:2]
    steps = noisy.shape[1]
    shape = jax.ShapeDtypeStruct
    ext = shape((2, steps + 2 * HALO, 8 * shots), f32)
    built = (
        shape((5, 64, 128), f32), shape((2, 64, 128), f32), shape((2, 256, 576), bf16),
        shape((16, 256), bf16),
    )
    outs = (ext, ext, shape((spans, 2, 128), f32)) + built
    dma = pltpu.SemaphoreType.DMA
    staged = [args[i] for i in (2, 3, 4, 5, 6, 7, 8, 9)]
    hbm = pl.BlockSpec(memory_space=pltpu.HBM)
    return pl.pallas_call(
        lambda *refs: exchange_kernel(shots, spans, *refs),
        out_shape=outs,
        in_specs=[hbm] * len(args),
        out_specs=(hbm,) * len(outs),
        scratch_shapes=[
            pltpu.VMEM((shots, 2, 8, steps), f32),
            pltpu.VMEM((2, 128), f32),
            pltpu.VMEM((2, steps, 128), f32),
        ] + [pltpu.VMEM(a.shape, a.dtype) for a in built] + [pltpu.VMEM(a.shape, a.dtype) for a in staged] + [
            dma((10,)), dma((6,)), dma((shots,)), dma((shots,)), dma((4,)), dma((4,)), dma((spans,)), dma((spans,)),
        ],
        compiler_params=pltpu.CompilerParams(
            collective_id=0, has_side_effects=True, vmem_limit_bytes=58 * 2**20
        ),
        name="exchange",
    )(*args)


def gelu_of_half(h):
    u = h * (2 * TANH_SCALE + (8 * TANH_SCALE * TANH_CUBE) * (h * h))
    return (h + h * jnp.tanh(u)).astype(bf16)


def mm(a, b):
    return jnp.dot(a, b, preferred_element_type=f32)


def denoise_kernel(
    spans,
    dil_in, noisy_in, masked_in, shares_in, cols_in, shot_base_in, wt_in, ow_in, last_in, out,
    dil, noisy, masked, shares, cols, shot_base, wt, ow, last, sem, x1, x2, state, *sums
):
    steps = out.shape[1]
    total_time = spans * steps
    by = len(sums)
    pairs = [
        (dil_in, dil), (noisy_in, noisy), (masked_in, masked), (shares_in, shares), (cols_in, cols),
        (shot_base_in, shot_base), (wt_in, wt), (ow_in, ow), (last_in, last),
    ]
    loads = [pltpu.make_async_copy(a, b, sem.at[i]) for i, (a, b) in enumerate(pairs)]
    for copy in loads:
        copy.start()
    for copy in loads[:6]:
        copy.wait()
    d1, d2 = dil[0], dil[1]
    energy = jnp.sum(jnp.sum(shares[...], axis=0), axis=1, keepdims=True)
    scale = lax.rsqrt(jnp.broadcast_to(energy, (2, 128)) / (total_time * 128) + 1e-5)
    first = lax.axis_index("tm") * steps - HALO
    lane = lax.broadcasted_iota(jnp.int32, (64, 128), 1)
    zeros = jnp.zeros((64, 128), bf16)

    def put(ref, row, halves, d):
        halves = [a.astype(bf16) for a in halves]
        ref[row, 64:128, :] = jnp.concatenate(halves, 1)
        low = [jnp.where(lane >= d, pltpu.roll(a, d, 1), zeros) for a in halves]
        ref[row, 0:64, :] = jnp.concatenate(low, 1)
        high = [jnp.where(lane < 128 - d, pltpu.roll(a, 128 - d, 1), zeros) for a in halves]
        ref[row, 128:192, :] = jnp.concatenate(high, 1)

    def norm(a, g, row):
        time = row + first
        inside = jnp.where(jnp.logical_and(time >= 0, time < total_time), 1.0, 0.0).astype(f32)
        mean_square = jnp.sum(a * a, axis=0, keepdims=True) * (1.0 / 64)
        return a * (lax.rsqrt(mean_square + 1e-5) * inside) * g

    def lift_row(row):
        source = jnp.minimum(row, noisy.shape[1] - 1)
        normed = []
        for s in range(2):
            a = cols[0] * noisy[s, pl.ds(source, 1), :]
            a = a + cols[1] * (masked[s, pl.ds(source, 1), :] * scale[s : s + 1]) + shot_base[s]
            state[row, :, s * 128 : (s + 1) * 128] = a
            normed.append(norm(a, cols[2], row))
        put(x1, row, normed, d1)

    def conv(l, ref, r, d):
        return mm(wt[l], jnp.concatenate([ref[r - d], ref[r], ref[r + d]], 0))

    start = HALO - d2
    trips = (steps + 2 * d2 + by - 1) // by
    ahead = start - d1

    def lifts(q, carry):
        for u in range(by):
            lift_row(ahead + q * by + u)
        return carry

    before = (2 * d1 + by + by - 1) // by
    lax.fori_loop(0, before, lifts, 0)
    lifted = ahead + before * by
    for copy in loads[6:]:
        copy.wait()
    for u in range(by):
        sums[u][...] = conv(0, x1, start + u, d1)
    for u in range(by):
        lift_row(lifted + u)
    lifted = lifted + by

    def first_end(r, act):
        updated = state[r] + mm(ow[0], act)
        state[r] = updated
        put(x2, r - DMAX, [norm(updated[:, s * 128 : (s + 1) * 128], cols[3], r) for s in range(2)], d2)

    def second_end(r, act):
        y = mm(last[...], act)
        y = y[0:1, :] + y[1:2, :]
        for s in range(2):
            lanes = slice(s * 128, (s + 1) * 128)
            h = jnp.sum(state[r + HALO, :, lanes] * cols[4], axis=0, keepdims=True)
            out[s, pl.ds(r, 1), :] = h + y[:, lanes]

    def first_block(q, carry):
        r = start + q * by
        for u in range(by):
            act = gelu_of_half(sums[u][...])
            sums[u][...] = conv(0, x1, r + by + u, d1)
            first_end(r + u, act)
        for u in range(by):
            lift_row(lifted + q * by + u)
        return carry

    lax.fori_loop(0, trips - 1, first_block, 0)
    r = start + (trips - 1) * by
    for u in range(by):
        act = gelu_of_half(sums[u][...])
        sums[u][...] = conv(1, x2, DMAX + u, d2)
        first_end(r + u, act)

    def second_block(q, carry):
        r = q * by
        for u in range(by):
            act = gelu_of_half(sums[u][...])
            sums[u][...] = conv(1, x2, DMAX + r + by + u, d2)
            second_end(r + u, act)
        return carry

    lax.fori_loop(0, steps // by - 1, second_block, 0)
    for u in range(by):
        second_end(steps - by + u, gelu_of_half(sums[u][...]))


def denoise(spans, dil, *args):
    steps = args[0].shape[1] - 2 * HALO
    hbm = pl.BlockSpec(memory_space=pltpu.HBM)
    return pl.pallas_call(
        lambda *refs: denoise_kernel(spans, *refs),
        out_shape=jax.ShapeDtypeStruct((2, steps, 128), f32),
        in_specs=[hbm] * (1 + len(args)),
        out_specs=pl.BlockSpec(memory_space=pltpu.VMEM),
        scratch_shapes=[pltpu.SMEM((2,), jnp.int32)] + [pltpu.VMEM(a.shape, a.dtype) for a in args] + [
            pltpu.SemaphoreType.DMA((9,)),
            pltpu.VMEM((176, 192, 256), bf16),
            pltpu.VMEM((136, 192, 256), bf16),
            pltpu.VMEM((176, 64, 256), f32),
        ] + [pltpu.VMEM((256, 256), f32)] * UNROLL,
        compiler_params=pltpu.CompilerParams(vmem_limit_bytes=58 * 2**20),
        name="denoise",
    )(dil, *args)


def solution(mesh):
    shots, spans = mesh.shape["shot"], mesh.shape["tm"]

    def per_device(
        noisy_gather, observed, missing, noise_level, dilations, lift_weight, level_weight,
        norm_gain, conv_weight, out_weight, head_weight,
    ):
        projections = jnp.swapaxes(out_weight, 1, 2)
        masked, noisy, shares, cols, shot_base, wt, last = exchange_inputs(
            shots, spans, jnp.swapaxes(observed, 1, 2), noisy_gather, missing, noise_level[None, :],
            lift_weight, level_weight[None, :], norm_gain, conv_weight, projections, head_weight[None, :],
        )
        return denoise(spans, dilations, noisy, masked, shares, cols, shot_base, wt, projections, last)

    return jax.shard_map(
        per_device,
        mesh=mesh,
        in_specs=(
            P("shot", "tm", None), P(None, "tm", "shot"), P("shot", None), P("shot"),
            P(), P(), P(), P(), P(), P(), P(),
        ),
        out_specs=P("shot", "tm", None),
        check_vma=False,
    )
```

```python
import jax
import jax.numpy as jnp
from jax import lax
from jax.experimental import pallas as pl
from jax.experimental.pallas import tpu as pltpu
from jax.sharding import PartitionSpec as P

MESH = pl.DeviceIdType.MESH
DMAX = 16
HALO = 2 * DMAX
TANH_SCALE = 0.7978845608028654
TANH_CUBE = 0.044715
EARLY, JOINT, RING = 8, 12, 4
f32, bf16 = jnp.float32, jnp.bfloat16


def column(row):
    return jnp.broadcast_to(jnp.broadcast_to(row, (8, row.shape[1])).T[:, :1], (row.shape[1], 128))


def exchange_kernel(
    shots, spans,
    obs, noisy, missing, level, lift, levw, gain, cw, ow, head,
    masked_ext, noisy_ext, sums, cols_out, shot_base_out, wt_out, last_out,
    landed, sent, masked, cols, shot_base, wt, last, miss, level_v, lift_v, levw_v, gain_v, cw_v, ow_v, head_v,
    local_sem, out_sem, shot_send, shot_recv, halo_send, halo_recv, sum_send, sum_recv,
):
    me_shot = lax.axis_index("shot")
    me_tm = lax.axis_index("tm")
    steps = noisy.shape[1]
    barrier = pltpu.get_barrier_semaphore()
    for step in range(1, shots):
        pl.semaphore_signal(
            barrier, inc=1, device_id={"shot": lax.rem(me_shot + step, shots)}, device_id_type=MESH
        )
    for step in range(1, spans):
        pl.semaphore_signal(
            barrier, inc=1, device_id={"tm": lax.rem(me_tm + step, spans)}, device_id_type=MESH
        )
    pairs = [
        (cw, cw_v), (ow, ow_v), (lift, lift_v), (levw, levw_v), (gain, gain_v), (head, head_v),
        (level, level_v), (missing, miss),
        (noisy, noisy_ext.at[:, pl.ds(HALO, steps), :]),
        (obs.at[pl.ds(2 * me_shot, 2)], landed.at[me_shot]),
    ]
    local = [pltpu.make_async_copy(a, b, local_sem.at[i]) for i, (a, b) in enumerate(pairs)]
    for copy in local:
        copy.start()
    pl.semaphore_wait(barrier, shots + spans - 2)

    right = {"tm": lax.rem(me_tm + 1, spans)}
    left = {"tm": lax.rem(me_tm + spans - 1, spans)}

    def halo(source, first, target, slot):
        up = pltpu.make_async_remote_copy(
            src_ref=source.at[:, pl.ds(first + steps - HALO, HALO), :],
            dst_ref=target.at[:, pl.ds(0, HALO), :],
            send_sem=halo_send.at[slot], recv_sem=halo_recv.at[slot],
            device_id=right, device_id_type=MESH,
        )
        down = pltpu.make_async_remote_copy(
            src_ref=source.at[:, pl.ds(first, HALO), :],
            dst_ref=target.at[:, pl.ds(HALO + steps, HALO), :],
            send_sem=halo_send.at[slot + 1], recv_sem=halo_recv.at[slot + 1],
            device_id=left, device_id_type=MESH,
        )
        up.start()
        down.start()
        return [up, down]

    exchange = []
    for step in range(1, shots):
        other = lax.rem(me_shot + step, shots)
        copy = pltpu.make_async_remote_copy(
            src_ref=obs.at[pl.ds(2 * other, 2)], dst_ref=landed.at[me_shot],
            send_sem=shot_send.at[step], recv_sem=shot_recv.at[step],
            device_id={"shot": other}, device_id_type=MESH,
        )
        copy.start()
        exchange.append(copy)
    halos = halo(noisy, 0, noisy_ext, 0)
    for copy in local:
        copy.wait()

    taps = cw.shape[1]
    for l in range(2):
        for k in range(0, taps, 2):
            count = min(2, taps - k)
            block = jnp.concatenate([cw_v[l, k + i] for i in range(count)], 0).astype(f32) * 0.5
            wt[l, :, k * 64 : (k + count) * 64] = block.T.astype(bf16)
    folded = lax.dot_general(
        head_v[...], ow_v[1].astype(f32), (((1,), (0,)), ((), ())), precision=lax.Precision.HIGHEST
    )
    high = folded.astype(bf16)
    low = (folded - high.astype(f32)).astype(bf16)
    last[...] = jnp.concatenate([high, low, jnp.zeros((14, 256), bf16)], 0)
    cols[0] = column(lift_v[0:1, :])
    cols[1] = column(lift_v[1:2, :])
    cols[2] = column(gain_v[0:1, :])
    cols[3] = column(gain_v[1:2, :])
    cols[4] = column(head_v[...])
    present = (1 - miss[...]).astype(f32)
    for s in range(2):
        noise = jnp.broadcast_to(level_v[0:1, s : s + 1], (64, 128))
        shot_base[s] = column(lift_v[2:3, :]) * present[s : s + 1, :] + noise * column(levw_v[...])

    results = [
        pltpu.make_async_copy(a, b, out_sem.at[i])
        for i, (a, b) in enumerate([(cols, cols_out), (shot_base, shot_base_out), (wt, wt_out), (last, last_out)])
    ]
    for copy in results:
        copy.start()

    for copy in exchange:
        copy.wait_recv()
    for s in range(2):
        rows = landed[:, s].reshape(8 * shots, steps).T * present[s : s + 1, :]
        masked[s] = rows
        sent[s : s + 1, :] = jnp.sum(rows * rows, axis=0, keepdims=True)
    sharing = []
    for step in range(1, spans):
        other = lax.rem(me_tm + step, spans)
        copy = pltpu.make_async_remote_copy(
            src_ref=sent, dst_ref=sums.at[me_tm],
            send_sem=sum_send.at[step], recv_sem=sum_recv.at[step],
            device_id={"tm": other}, device_id_type=MESH,
        )
        copy.start()
        sharing.append(copy)
    halos += halo(masked, 0, masked_ext, 2)
    mine = [
        pltpu.make_async_copy(sent, sums.at[me_tm], out_sem.at[4]),
        pltpu.make_async_copy(masked, masked_ext.at[:, pl.ds(HALO, steps), :], out_sem.at[5]),
    ]
    for copy in mine:
        copy.start()
    for copy in exchange:
        copy.wait_send()
    for copy in results + mine:
        copy.wait()
    for copy in sharing + halos:
        copy.wait()


def exchange_inputs(shots, spans, *args):
    obs, noisy = args[:2]
    steps = noisy.shape[1]
    shape = jax.ShapeDtypeStruct
    ext = shape((2, steps + 2 * HALO, 8 * shots), f32)
    built = (
        shape((5, 64, 128), f32), shape((2, 64, 128), f32), shape((2, 256, 576), bf16),
        shape((16, 256), bf16),
    )
    outs = (ext, ext, shape((spans, 2, 128), f32)) + built
    dma = pltpu.SemaphoreType.DMA
    staged = [args[i] for i in (2, 3, 4, 5, 6, 7, 8, 9)]
    hbm = pl.BlockSpec(memory_space=pltpu.HBM)
    return pl.pallas_call(
        lambda *refs: exchange_kernel(shots, spans, *refs),
        out_shape=outs,
        in_specs=[hbm] * len(args),
        out_specs=(hbm,) * len(outs),
        scratch_shapes=[
            pltpu.VMEM((shots, 2, 8, steps), f32),
            pltpu.VMEM((2, 128), f32),
            pltpu.VMEM((2, steps, 128), f32),
        ] + [pltpu.VMEM(a.shape, a.dtype) for a in built] + [pltpu.VMEM(a.shape, a.dtype) for a in staged] + [
            dma((10,)), dma((6,)), dma((shots,)), dma((shots,)), dma((4,)), dma((4,)), dma((spans,)), dma((spans,)),
        ],
        compiler_params=pltpu.CompilerParams(
            collective_id=0, has_side_effects=True, vmem_limit_bytes=58 * 2**20
        ),
        name="exchange",
    )(*args)


def gelu_of_half(h):
    u = h * (2 * TANH_SCALE + (8 * TANH_SCALE * TANH_CUBE) * (h * h))
    return (h + h * jnp.tanh(u)).astype(bf16)


def mm(a, b):
    return jnp.dot(a, b, preferred_element_type=f32)


def denoise_kernel(
    spans,
    dil_in, noisy_in, masked_in, shares_in, cols_in, shot_base_in, wt_in, ow_in, last_in, out,
    dil, noisy, masked, shares, cols, shot_base, wt, ow, last, sem, x1, x2, state, heads, *sums
):
    steps = out.shape[1]
    total_time = spans * steps
    sums1, sums2 = sums[:RING], sums[RING:]
    pairs = [
        (dil_in, dil), (noisy_in, noisy), (masked_in, masked), (shares_in, shares), (cols_in, cols),
        (shot_base_in, shot_base), (wt_in, wt), (ow_in, ow), (last_in, last),
    ]
    loads = [pltpu.make_async_copy(a, b, sem.at[i]) for i, (a, b) in enumerate(pairs)]
    for copy in loads:
        copy.start()
    for copy in loads[:6]:
        copy.wait()
    d1, d2 = dil[0], dil[1]
    energy = jnp.sum(jnp.sum(shares[...], axis=0), axis=1, keepdims=True)
    scale = lax.rsqrt(jnp.broadcast_to(energy, (2, 128)) / (total_time * 128) + 1e-5)
    first = lax.axis_index("tm") * steps - HALO
    lane = lax.broadcasted_iota(jnp.int32, (64, 128), 1)
    zeros = jnp.zeros((64, 128), bf16)

    def put(ref, row, halves, d):
        halves = [a.astype(bf16) for a in halves]
        ref[row, 64:128, :] = jnp.concatenate(halves, 1)
        low = [jnp.where(lane >= d, pltpu.roll(a, d, 1), zeros) for a in halves]
        ref[row, 0:64, :] = jnp.concatenate(low, 1)
        high = [jnp.where(lane < 128 - d, pltpu.roll(a, 128 - d, 1), zeros) for a in halves]
        ref[row, 128:192, :] = jnp.concatenate(high, 1)

    def norm(a, g, row):
        time = row + first
        inside = jnp.where(jnp.logical_and(time >= 0, time < total_time), 1.0, 0.0).astype(f32)
        mean_square = jnp.sum(a * a, axis=0, keepdims=True) * (1.0 / 64)
        return a * (lax.rsqrt(mean_square + 1e-5) * inside) * g

    def lift_row(row):
        source = jnp.minimum(row, noisy.shape[1] - 1)
        normed = []
        for s in range(2):
            a = cols[0] * noisy[s, pl.ds(source, 1), :]
            a = a + cols[1] * (masked[s, pl.ds(source, 1), :] * scale[s : s + 1]) + shot_base[s]
            state[row, :, s * 128 : (s + 1) * 128] = a
            normed.append(norm(a, cols[2], row))
        put(x1, row, normed, d1)

    def conv(l, ref, r, d):
        return mm(wt[l], jnp.concatenate([ref[r - d], ref[r], ref[r + d]], 0))

    lead = RING + JOINT + d2
    early = (lead + d2 + EARLY - 1) // EARLY
    start = HALO + lead - early * EARLY
    ahead = start - d1

    def lifts(q, carry):
        for u in range(8):
            lift_row(ahead + q * 8 + u)
        return carry

    before = (2 * d1 + RING + JOINT + 7) // 8
    lax.fori_loop(0, before, lifts, 0)
    lifted = ahead + before * 8
    for copy in loads[6:]:
        copy.wait()
    for u in range(RING):
        sums1[u][...] = conv(0, x1, start + u, d1)

    def first_end(r, act):
        updated = state[r] + mm(ow[0], act)
        halves = [updated[:, s * 128 : (s + 1) * 128] for s in range(2)]
        heads[r] = jnp.concatenate([jnp.sum(a * cols[4], axis=0, keepdims=True) for a in halves], 1)
        put(x2, r - DMAX, [norm(a, cols[3], r) for a in halves], d2)

    def second_end(r, act):
        y = mm(last[...], act)
        y = y[0:1, :] + y[1:2, :] + heads[r + HALO]
        for s in range(2):
            out[s, pl.ds(r, 1), :] = y[:, s * 128 : (s + 1) * 128]

    def first_block(r, count):
        for u in range(count):
            act = gelu_of_half(sums1[u % RING][...])
            sums1[u % RING][...] = conv(0, x1, r + RING + u, d1)
            first_end(r + u, act)

    def second_block(r, count, lift_from=None):
        for u in range(count):
            act = gelu_of_half(sums2[u % RING][...])
            sums2[u % RING][...] = conv(1, x2, DMAX + r + RING + u, d2)
            second_end(r + u, act)
            if lift_from is not None:
                lift_row(lift_from + u)

    def alone(q, carry):
        first_block(start + q * EARLY, EARLY)
        for u in range(EARLY):
            lift_row(lifted + q * EARLY + u)
        return carry

    lax.fori_loop(0, early, alone, 0)
    for u in range(RING):
        sums2[u][...] = conv(1, x2, DMAX + u, d2)

    def joint(q, carry):
        second_block(q * JOINT, JOINT, lifted + early * EARLY + q * JOINT)
        first_block(HALO + lead + q * JOINT, JOINT)
        return carry

    trips = (steps - RING - JOINT) // JOINT
    lax.fori_loop(0, trips, joint, 0)
    second_block(trips * JOINT, JOINT)
    for u in range(RING):
        second_end(steps - RING + u, gelu_of_half(sums2[u][...]))


def denoise(spans, dil, *args):
    steps = args[0].shape[1] - 2 * HALO
    hbm = pl.BlockSpec(memory_space=pltpu.HBM)
    return pl.pallas_call(
        lambda *refs: denoise_kernel(spans, *refs),
        out_shape=jax.ShapeDtypeStruct((2, steps, 128), f32),
        in_specs=[hbm] * (1 + len(args)),
        out_specs=pl.BlockSpec(memory_space=pltpu.VMEM),
        scratch_shapes=[pltpu.SMEM((2,), jnp.int32)] + [pltpu.VMEM(a.shape, a.dtype) for a in args] + [
            pltpu.SemaphoreType.DMA((9,)),
            pltpu.VMEM((160, 192, 256), bf16),
            pltpu.VMEM((112, 192, 256), bf16),
            pltpu.VMEM((160, 64, 256), f32),
            pltpu.VMEM((128, 1, 256), f32),
        ] + [pltpu.VMEM((256, 256), f32)] * (2 * RING),
        compiler_params=pltpu.CompilerParams(vmem_limit_bytes=58 * 2**20),
        name="denoise",
    )(dil, *args)


def solution(mesh):
    shots, spans = mesh.shape["shot"], mesh.shape["tm"]

    def per_device(
        noisy_gather, observed, missing, noise_level, dilations, lift_weight, level_weight,
        norm_gain, conv_weight, out_weight, head_weight,
    ):
        projections = jnp.swapaxes(out_weight, 1, 2)
        masked, noisy, shares, cols, shot_base, wt, last = exchange_inputs(
            shots, spans, jnp.swapaxes(observed, 1, 2), noisy_gather, missing, noise_level[None, :],
            lift_weight, level_weight[None, :], norm_gain, conv_weight, projections, head_weight[None, :],
        )
        return denoise(spans, dilations, noisy, masked, shares, cols, shot_base, wt, projections, last)

    return jax.shard_map(
        per_device,
        mesh=mesh,
        in_specs=(
            P("shot", "tm", None), P(None, "tm", "shot"), P("shot", None), P("shot"),
            P(), P(), P(), P(), P(), P(), P(),
        ),
        out_specs=P("shot", "tm", None),
        check_vma=False,
    )
```

```python
import jax
import jax.numpy as jnp
from jax import lax
from jax.experimental import pallas as pl
from jax.experimental.pallas import tpu as pltpu
from jax.sharding import PartitionSpec as P

MESH = pl.DeviceIdType.MESH
DMAX = 16
HALO = 2 * DMAX
TANH_SCALE = 0.7978845608028654
TANH_CUBE = 0.044715
EARLY, JOINT, RING, LIFTS = 12, 12, 4, 9
f32, bf16 = jnp.float32, jnp.bfloat16


def column(row):
    return jnp.broadcast_to(jnp.broadcast_to(row, (8, row.shape[1])).T[:, :1], (row.shape[1], 128))


def exchange_kernel(
    shots, spans,
    obs, noisy, missing, level, lift, levw, gain, cw, ow, head,
    masked_ext, noisy_ext, sums, cols_out, shot_base_out, wt_out, last_out,
    landed, obs_v, packed, sent, masked, cols, shot_base, wt, last, miss, level_v, lift_v, levw_v, gain_v, cw_v, ow_v, head_v,
    local_sem, out_sem, shot_send, shot_recv, halo_send, halo_recv, sum_send, sum_recv,
):
    me_shot = lax.axis_index("shot")
    me_tm = lax.axis_index("tm")
    steps = noisy.shape[1]
    barrier = pltpu.get_barrier_semaphore()
    for step in range(1, shots):
        pl.semaphore_signal(
            barrier, inc=1, device_id={"shot": lax.rem(me_shot + step, shots)}, device_id_type=MESH
        )
    for step in range(1, spans):
        pl.semaphore_signal(
            barrier, inc=1, device_id={"tm": lax.rem(me_tm + step, spans)}, device_id_type=MESH
        )
    pairs = [
        (cw, cw_v), (ow, ow_v), (lift, lift_v), (levw, levw_v), (gain, gain_v), (head, head_v),
        (level, level_v), (missing, miss),
        (noisy, noisy_ext.at[:, pl.ds(HALO, steps), :]),
        (obs, obs_v),
    ]
    local = [pltpu.make_async_copy(a, b, local_sem.at[i]) for i, (a, b) in enumerate(pairs)]
    for copy in local:
        copy.start()
    local.pop().wait()
    for k in range(shots):
        packed[k] = jnp.concatenate([obs_v[2 * k], obs_v[2 * k + 1]], 1)
    landed[me_shot] = packed[me_shot]
    pl.semaphore_wait(barrier, shots + spans - 2)

    right = {"tm": lax.rem(me_tm + 1, spans)}
    left = {"tm": lax.rem(me_tm + spans - 1, spans)}

    def halo(source, first, target, slot):
        up = pltpu.make_async_remote_copy(
            src_ref=source.at[:, pl.ds(first + steps - HALO, HALO), :],
            dst_ref=target.at[:, pl.ds(0, HALO), :],
            send_sem=halo_send.at[slot], recv_sem=halo_recv.at[slot],
            device_id=right, device_id_type=MESH,
        )
        down = pltpu.make_async_remote_copy(
            src_ref=source.at[:, pl.ds(first, HALO), :],
            dst_ref=target.at[:, pl.ds(HALO + steps, HALO), :],
            send_sem=halo_send.at[slot + 1], recv_sem=halo_recv.at[slot + 1],
            device_id=left, device_id_type=MESH,
        )
        up.start()
        down.start()
        return [up, down]

    exchange = []
    for step in range(1, shots):
        other = lax.rem(me_shot + step, shots)
        copy = pltpu.make_async_remote_copy(
            src_ref=packed.at[other], dst_ref=landed.at[me_shot],
            send_sem=shot_send.at[step], recv_sem=shot_recv.at[step],
            device_id={"shot": other}, device_id_type=MESH,
        )
        copy.start()
        exchange.append(copy)
    halos = halo(noisy, 0, noisy_ext, 0)
    for copy in local:
        copy.wait()

    taps = cw.shape[1]
    for l in range(2):
        for k in range(0, taps, 2):
            count = min(2, taps - k)
            block = jnp.concatenate([cw_v[l, k + i] for i in range(count)], 0).astype(f32) * 0.5
            wt[l, :, k * 64 : (k + count) * 64] = block.T.astype(bf16)
    folded = lax.dot_general(
        head_v[...], ow_v[1].astype(f32), (((1,), (0,)), ((), ())), precision=lax.Precision.HIGHEST
    )
    high = folded.astype(bf16)
    low = (folded - high.astype(f32)).astype(bf16)
    last[...] = jnp.concatenate([high, low, jnp.zeros((14, 256), bf16)], 0)
    cols[0] = column(lift_v[0:1, :])
    cols[1] = column(lift_v[1:2, :])
    cols[2] = column(gain_v[0:1, :])
    cols[3] = column(gain_v[1:2, :])
    cols[4] = column(head_v[...])
    present = (1 - miss[...]).astype(f32)
    for s in range(2):
        noise = jnp.broadcast_to(level_v[0:1, s : s + 1], (64, 128))
        shot_base[s] = column(lift_v[2:3, :]) * present[s : s + 1, :] + noise * column(levw_v[...])

    results = [
        pltpu.make_async_copy(a, b, out_sem.at[i])
        for i, (a, b) in enumerate([(cols, cols_out), (shot_base, shot_base_out), (wt, wt_out), (last, last_out)])
    ]
    for copy in results:
        copy.start()

    for copy in exchange:
        copy.wait_recv()
    arrived = landed[...].reshape(8 * shots, 2 * steps).T
    for s in range(2):
        rows = arrived[s * steps : (s + 1) * steps] * present[s : s + 1, :]
        masked[s] = rows
        sent[s : s + 1, :] = jnp.sum(rows * rows, axis=0, keepdims=True)
    sharing = []
    for step in range(1, spans):
        other = lax.rem(me_tm + step, spans)
        copy = pltpu.make_async_remote_copy(
            src_ref=sent, dst_ref=sums.at[me_tm],
            send_sem=sum_send.at[step], recv_sem=sum_recv.at[step],
            device_id={"tm": other}, device_id_type=MESH,
        )
        copy.start()
        sharing.append(copy)
    halos += halo(masked, 0, masked_ext, 2)
    mine = [
        pltpu.make_async_copy(sent, sums.at[me_tm], out_sem.at[4]),
        pltpu.make_async_copy(masked, masked_ext.at[:, pl.ds(HALO, steps), :], out_sem.at[5]),
    ]
    for copy in mine:
        copy.start()
    for copy in exchange:
        copy.wait_send()
    for copy in results + mine:
        copy.wait()
    for copy in sharing + halos:
        copy.wait()


def exchange_inputs(shots, spans, *args):
    obs, noisy = args[:2]
    steps = noisy.shape[1]
    shape = jax.ShapeDtypeStruct
    ext = shape((2, steps + 2 * HALO, 8 * shots), f32)
    built = (
        shape((5, 64, 128), f32), shape((2, 64, 128), f32), shape((2, 256, 576), bf16),
        shape((16, 256), bf16),
    )
    outs = (ext, ext, shape((spans, 2, 128), f32)) + built
    dma = pltpu.SemaphoreType.DMA
    staged = [args[i] for i in (2, 3, 4, 5, 6, 7, 8, 9)]
    hbm = pl.BlockSpec(memory_space=pltpu.HBM)
    return pl.pallas_call(
        lambda *refs: exchange_kernel(shots, spans, *refs),
        out_shape=outs,
        in_specs=[hbm] * len(args),
        out_specs=(hbm,) * len(outs),
        scratch_shapes=[
            pltpu.VMEM((shots, 8, 2 * steps), f32),
            pltpu.VMEM(obs.shape, f32),
            pltpu.VMEM((shots, 8, 2 * steps), f32),
            pltpu.VMEM((2, 128), f32),
            pltpu.VMEM((2, steps, 128), f32),
        ] + [pltpu.VMEM(a.shape, a.dtype) for a in built] + [pltpu.VMEM(a.shape, a.dtype) for a in staged] + [
            dma((10,)), dma((6,)), dma((shots,)), dma((shots,)), dma((4,)), dma((4,)), dma((spans,)), dma((spans,)),
        ],
        compiler_params=pltpu.CompilerParams(
            collective_id=0, has_side_effects=True, vmem_limit_bytes=58 * 2**20
        ),
        name="exchange",
    )(*args)


def gelu_of_half(h):
    u = h * (2 * TANH_SCALE + (8 * TANH_SCALE * TANH_CUBE) * (h * h))
    return (h + h * jnp.tanh(u)).astype(bf16)


def mm(a, b):
    return jnp.dot(a, b, preferred_element_type=f32)


def denoise_kernel(
    spans,
    dil_in, noisy_in, masked_in, shares_in, cols_in, shot_base_in, wt_in, ow_in, last_in, out,
    dil, noisy, masked, shares, cols, shot_base, wt, ow, last, sem, x1, x2, state, heads, *sums
):
    steps = out.shape[1]
    total_time = spans * steps
    sums1, sums2 = sums[:RING], sums[RING:]
    pairs = [
        (dil_in, dil), (noisy_in, noisy), (masked_in, masked), (shares_in, shares), (cols_in, cols),
        (shot_base_in, shot_base), (wt_in, wt), (ow_in, ow), (last_in, last),
    ]
    loads = [pltpu.make_async_copy(a, b, sem.at[i]) for i, (a, b) in enumerate(pairs)]
    for copy in loads:
        copy.start()
    for copy in loads[:6]:
        copy.wait()
    d1, d2 = dil[0], dil[1]
    energy = jnp.sum(jnp.sum(shares[...], axis=0), axis=1, keepdims=True)
    scale = lax.rsqrt(jnp.broadcast_to(energy, (2, 128)) / (total_time * 128) + 1e-5)
    first = lax.axis_index("tm") * steps - HALO
    lane = lax.broadcasted_iota(jnp.int32, (64, 128), 1)
    zeros = jnp.zeros((64, 128), bf16)

    def put(ref, row, halves, d):
        halves = [a.astype(bf16) for a in halves]
        ref[row, 64:128, :] = jnp.concatenate(halves, 1)
        low = [jnp.where(lane >= d, pltpu.roll(a, d, 1), zeros) for a in halves]
        ref[row, 0:64, :] = jnp.concatenate(low, 1)
        high = [jnp.where(lane < 128 - d, pltpu.roll(a, 128 - d, 1), zeros) for a in halves]
        ref[row, 128:192, :] = jnp.concatenate(high, 1)

    def norm(a, g, row):
        time = row + first
        inside = jnp.where(jnp.logical_and(time >= 0, time < total_time), 1.0, 0.0).astype(f32)
        mean_square = jnp.sum(a * a, axis=0, keepdims=True) * (1.0 / 64)
        return a * (lax.rsqrt(mean_square + 1e-5) * inside) * g

    def lift_row(row):
        source = jnp.minimum(row, noisy.shape[1] - 1)
        normed = []
        for s in range(2):
            a = cols[0] * noisy[s, pl.ds(source, 1), :]
            a = a + cols[1] * (masked[s, pl.ds(source, 1), :] * scale[s : s + 1]) + shot_base[s]
            state[row, :, s * 128 : (s + 1) * 128] = a
            normed.append(norm(a, cols[2], row))
        put(x1, row, normed, d1)

    def conv(l, ref, r, d):
        return mm(wt[l], jnp.concatenate([ref[r - d], ref[r], ref[r + d]], 0))

    lead = RING + JOINT + d2
    early = (lead + d2 + EARLY - 1) // EARLY
    start = HALO + lead - early * EARLY
    ahead = start - d1

    def lifts(q, carry):
        for u in range(8):
            lift_row(ahead + q * 8 + u)
        return carry

    before = (2 * d1 + RING + JOINT + 7) // 8
    lax.fori_loop(0, before, lifts, 0)
    lifted = ahead + before * 8
    for copy in loads[6:]:
        copy.wait()
    for u in range(RING):
        sums1[u][...] = conv(0, x1, start + u, d1)

    def first_end(r, act):
        updated = state[r] + mm(ow[0], act)
        halves = [updated[:, s * 128 : (s + 1) * 128] for s in range(2)]
        heads[r] = jnp.concatenate([jnp.sum(a * cols[4], axis=0, keepdims=True) for a in halves], 1)
        put(x2, r - DMAX, [norm(a, cols[3], r) for a in halves], d2)

    def second_end(r, act):
        y = mm(last[...], act)
        y = y[0:1, :] + y[1:2, :] + heads[r + HALO]
        for s in range(2):
            out[s, pl.ds(r, 1), :] = y[:, s * 128 : (s + 1) * 128]

    def first_block(r, count):
        for u in range(count):
            act = gelu_of_half(sums1[u % RING][...])
            sums1[u % RING][...] = conv(0, x1, r + RING + u, d1)
            first_end(r + u, act)

    def second_block(r, count, lift_from=None):
        for u in range(count):
            act = gelu_of_half(sums2[u % RING][...])
            sums2[u % RING][...] = conv(1, x2, DMAX + r + RING + u, d2)
            second_end(r + u, act)
            if lift_from is not None and u < LIFTS:
                lift_row(lift_from + u)

    def alone(q, carry):
        first_block(start + q * EARLY, EARLY)
        for u in range(EARLY):
            lift_row(lifted + q * EARLY + u)
        return carry

    lax.fori_loop(0, early, alone, 0)
    for u in range(RING):
        sums2[u][...] = conv(1, x2, DMAX + u, d2)

    def joint(q, carry):
        second_block(q * JOINT, JOINT, lifted + early * EARLY + q * LIFTS)
        first_block(HALO + lead + q * JOINT, JOINT)
        return carry

    trips = (steps - RING - JOINT) // JOINT
    lax.fori_loop(0, trips, joint, 0)
    second_block(trips * JOINT, JOINT)
    for u in range(RING):
        second_end(steps - RING + u, gelu_of_half(sums2[u][...]))


def denoise(spans, dil, *args):
    steps = args[0].shape[1] - 2 * HALO
    hbm = pl.BlockSpec(memory_space=pltpu.HBM)
    return pl.pallas_call(
        lambda *refs: denoise_kernel(spans, *refs),
        out_shape=jax.ShapeDtypeStruct((2, steps, 128), f32),
        in_specs=[hbm] * (1 + len(args)),
        out_specs=pl.BlockSpec(memory_space=pltpu.VMEM),
        scratch_shapes=[pltpu.SMEM((2,), jnp.int32)] + [pltpu.VMEM(a.shape, a.dtype) for a in args] + [
            pltpu.SemaphoreType.DMA((9,)),
            pltpu.VMEM((160, 192, 256), bf16),
            pltpu.VMEM((112, 192, 256), bf16),
            pltpu.VMEM((160, 64, 256), f32),
            pltpu.VMEM((128, 1, 256), f32),
        ] + [pltpu.VMEM((256, 256), f32)] * (2 * RING),
        compiler_params=pltpu.CompilerParams(vmem_limit_bytes=58 * 2**20),
        name="denoise",
    )(dil, *args)


def solution(mesh):
    shots, spans = mesh.shape["shot"], mesh.shape["tm"]

    def per_device(
        noisy_gather, observed, missing, noise_level, dilations, lift_weight, level_weight,
        norm_gain, conv_weight, out_weight, head_weight,
    ):
        projections = jnp.swapaxes(out_weight, 1, 2)
        masked, noisy, shares, cols, shot_base, wt, last = exchange_inputs(
            shots, spans, jnp.swapaxes(observed, 1, 2), noisy_gather, missing, noise_level[None, :],
            lift_weight, level_weight[None, :], norm_gain, conv_weight, projections, head_weight[None, :],
        )
        return denoise(spans, dilations, noisy, masked, shares, cols, shot_base, wt, projections, last)

    return jax.shard_map(
        per_device,
        mesh=mesh,
        in_specs=(
            P("shot", "tm", None), P(None, "tm", "shot"), P("shot", None), P("shot"),
            P(), P(), P(), P(), P(), P(), P(),
        ),
        out_specs=P("shot", "tm", None),
        check_vma=False,
    )
```

```python
import jax
import jax.numpy as jnp
from jax import lax
from jax.experimental import pallas as pl
from jax.experimental.pallas import tpu as pltpu
from jax.sharding import PartitionSpec as P

MESH = pl.DeviceIdType.MESH
DMAX = 16
HALO = 2 * DMAX
TANH_SCALE = 0.7978845608028654
TANH_CUBE = 0.044715
EARLY, JOINT, RING, LIFTS = 12, 12, 4, 9
f32, bf16 = jnp.float32, jnp.bfloat16


def column(row):
    return jnp.broadcast_to(jnp.broadcast_to(row, (8, row.shape[1])).T[:, :1], (row.shape[1], 128))


def exchange_kernel(
    shots, spans,
    obs, noisy, missing, level, lift, levw, gain, cw, ow, head,
    masked_ext, noisy_ext, sums, cols_out, shot_base_out, wt_out, proj_out, last_out,
    landed, obs_v, packed, sent, masked, cols, shot_base, wt, proj, last, miss, level_v, lift_v, levw_v, gain_v, cw_v, ow_v, head_v,
    local_sem, out_sem, shot_send, shot_recv, halo_send, halo_recv, sum_send, sum_recv,
):
    me_shot = lax.axis_index("shot")
    me_tm = lax.axis_index("tm")
    steps = noisy.shape[1]
    barrier = pltpu.get_barrier_semaphore()
    for step in range(1, shots):
        pl.semaphore_signal(
            barrier, inc=1, device_id={"shot": lax.rem(me_shot + step, shots)}, device_id_type=MESH
        )
    for step in range(1, spans):
        pl.semaphore_signal(
            barrier, inc=1, device_id={"tm": lax.rem(me_tm + step, spans)}, device_id_type=MESH
        )
    pairs = [
        (cw, cw_v), (ow, ow_v), (lift, lift_v), (levw, levw_v), (gain, gain_v), (head, head_v),
        (level, level_v), (missing, miss),
        (noisy, noisy_ext.at[:, pl.ds(HALO, steps), :]),
        (obs, obs_v),
    ]
    local = [pltpu.make_async_copy(a, b, local_sem.at[i]) for i, (a, b) in enumerate(pairs)]
    for copy in local:
        copy.start()
    local.pop().wait()
    for k in range(shots):
        packed[k] = jnp.concatenate([obs_v[2 * k], obs_v[2 * k + 1]], 1)
    landed[me_shot] = packed[me_shot]
    pl.semaphore_wait(barrier, shots + spans - 2)

    right = {"tm": lax.rem(me_tm + 1, spans)}
    left = {"tm": lax.rem(me_tm + spans - 1, spans)}

    def halo(source, first, target, slot):
        up = pltpu.make_async_remote_copy(
            src_ref=source.at[:, pl.ds(first + steps - HALO, HALO), :],
            dst_ref=target.at[:, pl.ds(0, HALO), :],
            send_sem=halo_send.at[slot], recv_sem=halo_recv.at[slot],
            device_id=right, device_id_type=MESH,
        )
        down = pltpu.make_async_remote_copy(
            src_ref=source.at[:, pl.ds(first, HALO), :],
            dst_ref=target.at[:, pl.ds(HALO + steps, HALO), :],
            send_sem=halo_send.at[slot + 1], recv_sem=halo_recv.at[slot + 1],
            device_id=left, device_id_type=MESH,
        )
        up.start()
        down.start()
        return [up, down]

    exchange = []
    for step in range(1, shots):
        other = lax.rem(me_shot + step, shots)
        copy = pltpu.make_async_remote_copy(
            src_ref=packed.at[other], dst_ref=landed.at[me_shot],
            send_sem=shot_send.at[step], recv_sem=shot_recv.at[step],
            device_id={"shot": other}, device_id_type=MESH,
        )
        copy.start()
        exchange.append(copy)
    halos = halo(noisy, 0, noisy_ext, 0)
    for copy in local:
        copy.wait()

    taps = cw.shape[1]
    for l in range(2):
        for k in range(0, taps, 2):
            count = min(2, taps - k)
            block = jnp.concatenate([cw_v[l, k + i] for i in range(count)], 0).astype(f32) * 0.5
            wt[l, :, k * 64 : (k + count) * 64] = block.T.astype(bf16)
    for l, (ref, ahead) in enumerate([(proj, ow_v[0]), (last, None)]):
        folded = lax.dot_general(
            head_v[...], ow_v[l].astype(f32), (((1,), (0,)), ((), ())), precision=lax.Precision.HIGHEST
        )
        high = folded.astype(bf16)
        low = (folded - high.astype(f32)).astype(bf16)
        rows = [high, low, jnp.zeros((14, 256), bf16)]
        ref[...] = jnp.concatenate(rows if ahead is None else [ahead] + rows, 0)
    cols[0] = column(lift_v[0:1, :])
    cols[1] = column(lift_v[1:2, :])
    cols[2] = column(gain_v[0:1, :])
    cols[3] = column(gain_v[1:2, :])
    cols[4] = column(head_v[...])
    present = (1 - miss[...]).astype(f32)
    for s in range(2):
        noise = jnp.broadcast_to(level_v[0:1, s : s + 1], (64, 128))
        shot_base[s] = column(lift_v[2:3, :]) * present[s : s + 1, :] + noise * column(levw_v[...])

    results = [
        pltpu.make_async_copy(a, b, out_sem.at[i])
        for i, (a, b) in enumerate([(cols, cols_out), (shot_base, shot_base_out), (wt, wt_out), (proj, proj_out), (last, last_out)])
    ]
    for copy in results:
        copy.start()

    for copy in exchange:
        copy.wait_recv()
    arrived = landed[...].reshape(8 * shots, 2 * steps).T
    for s in range(2):
        rows = arrived[s * steps : (s + 1) * steps] * present[s : s + 1, :]
        masked[s] = rows
        sent[s : s + 1, :] = jnp.sum(rows * rows, axis=0, keepdims=True)
    sharing = []
    for step in range(1, spans):
        other = lax.rem(me_tm + step, spans)
        copy = pltpu.make_async_remote_copy(
            src_ref=sent, dst_ref=sums.at[me_tm],
            send_sem=sum_send.at[step], recv_sem=sum_recv.at[step],
            device_id={"tm": other}, device_id_type=MESH,
        )
        copy.start()
        sharing.append(copy)
    halos += halo(masked, 0, masked_ext, 2)
    mine = [
        pltpu.make_async_copy(sent, sums.at[me_tm], out_sem.at[5]),
        pltpu.make_async_copy(masked, masked_ext.at[:, pl.ds(HALO, steps), :], out_sem.at[6]),
    ]
    for copy in mine:
        copy.start()
    for copy in exchange:
        copy.wait_send()
    for copy in results + mine:
        copy.wait()
    for copy in sharing + halos:
        copy.wait()


def exchange_inputs(shots, spans, *args):
    obs, noisy = args[:2]
    steps = noisy.shape[1]
    shape = jax.ShapeDtypeStruct
    ext = shape((2, steps + 2 * HALO, 8 * shots), f32)
    built = (
        shape((5, 64, 128), f32), shape((2, 64, 128), f32), shape((2, 256, 576), bf16),
        shape((80, 256), bf16), shape((16, 256), bf16),
    )
    outs = (ext, ext, shape((spans, 2, 128), f32)) + built
    dma = pltpu.SemaphoreType.DMA
    staged = [args[i] for i in (2, 3, 4, 5, 6, 7, 8, 9)]
    hbm = pl.BlockSpec(memory_space=pltpu.HBM)
    return pl.pallas_call(
        lambda *refs: exchange_kernel(shots, spans, *refs),
        out_shape=outs,
        in_specs=[hbm] * len(args),
        out_specs=(hbm,) * len(outs),
        scratch_shapes=[
            pltpu.VMEM((shots, 8, 2 * steps), f32),
            pltpu.VMEM(obs.shape, f32),
            pltpu.VMEM((shots, 8, 2 * steps), f32),
            pltpu.VMEM((2, 128), f32),
            pltpu.VMEM((2, steps, 128), f32),
        ] + [pltpu.VMEM(a.shape, a.dtype) for a in built] + [pltpu.VMEM(a.shape, a.dtype) for a in staged] + [
            dma((10,)), dma((7,)), dma((shots,)), dma((shots,)), dma((4,)), dma((4,)), dma((spans,)), dma((spans,)),
        ],
        compiler_params=pltpu.CompilerParams(
            collective_id=0, has_side_effects=True, vmem_limit_bytes=58 * 2**20
        ),
        name="exchange",
    )(*args)


def gelu_of_half(h):
    u = h * (2 * TANH_SCALE + (8 * TANH_SCALE * TANH_CUBE) * (h * h))
    return (h + h * jnp.tanh(u)).astype(bf16)


def mm(a, b):
    return jnp.dot(a, b, preferred_element_type=f32)


def denoise_kernel(
    spans,
    dil_in, noisy_in, masked_in, shares_in, cols_in, shot_base_in, wt_in, proj_in, last_in, out,
    dil, noisy, masked, shares, cols, shot_base, wt, proj, last, sem, x1, x2, state, heads, *sums
):
    steps = out.shape[1]
    total_time = spans * steps
    sums1, sums2 = sums[:RING], sums[RING:]
    pairs = [
        (dil_in, dil), (noisy_in, noisy), (masked_in, masked), (shares_in, shares), (cols_in, cols),
        (shot_base_in, shot_base), (wt_in, wt), (proj_in, proj), (last_in, last),
    ]
    loads = [pltpu.make_async_copy(a, b, sem.at[i]) for i, (a, b) in enumerate(pairs)]
    for copy in loads:
        copy.start()
    for copy in loads[:6]:
        copy.wait()
    d1, d2 = dil[0], dil[1]
    energy = jnp.sum(jnp.sum(shares[...], axis=0), axis=1, keepdims=True)
    scale = lax.rsqrt(jnp.broadcast_to(energy, (2, 128)) / (total_time * 128) + 1e-5)
    first = lax.axis_index("tm") * steps - HALO
    head_noisy = jnp.sum(cols[4] * cols[0], axis=0, keepdims=True)
    head_masked = jnp.sum(cols[4] * cols[1], axis=0, keepdims=True)
    for s in range(2):
        head_base = jnp.sum(cols[4] * shot_base[s], axis=0, keepdims=True)
        own = pl.ds(HALO, steps)
        out[s] = head_noisy * noisy[s, own, :] + head_masked * scale[s : s + 1] * masked[s, own, :] + head_base
    lane = lax.broadcasted_iota(jnp.int32, (64, 128), 1)
    zeros = jnp.zeros((64, 128), bf16)

    def put(ref, row, halves, d):
        halves = [a.astype(bf16) for a in halves]
        ref[row, 64:128, :] = jnp.concatenate(halves, 1)
        low = [jnp.where(lane >= d, pltpu.roll(a, d, 1), zeros) for a in halves]
        ref[row, 0:64, :] = jnp.concatenate(low, 1)
        high = [jnp.where(lane < 128 - d, pltpu.roll(a, 128 - d, 1), zeros) for a in halves]
        ref[row, 128:192, :] = jnp.concatenate(high, 1)

    def norm(a, g, row):
        time = row + first
        inside = jnp.where(jnp.logical_and(time >= 0, time < total_time), 1.0, 0.0).astype(f32)
        mean_square = jnp.sum(a * a, axis=0, keepdims=True) * (1.0 / 64)
        return a * (lax.rsqrt(mean_square + 1e-5) * inside) * g

    def lift_row(row):
        source = jnp.minimum(row, noisy.shape[1] - 1)
        normed = []
        for s in range(2):
            a = cols[0] * noisy[s, pl.ds(source, 1), :]
            a = a + cols[1] * (masked[s, pl.ds(source, 1), :] * scale[s : s + 1]) + shot_base[s]
            state[row, :, s * 128 : (s + 1) * 128] = a
            normed.append(norm(a, cols[2], row))
        put(x1, row, normed, d1)

    def conv(l, ref, r, d):
        return mm(wt[l], jnp.concatenate([ref[r - d], ref[r], ref[r + d]], 0))

    lead = RING + JOINT + d2
    early = (lead + d2 + EARLY - 1) // EARLY
    start = HALO + lead - early * EARLY
    ahead = start - d1

    def lifts(q, carry):
        for u in range(8):
            lift_row(ahead + q * 8 + u)
        return carry

    before = (2 * d1 + RING + JOINT + 7) // 8 - 1
    lax.fori_loop(0, before, lifts, 0)
    lifted = ahead + before * 8
    for copy in loads[6:]:
        copy.wait()
    for u in range(RING):
        sums1[u][...] = conv(0, x1, start + u, d1)
    for u in range(8):
        lift_row(lifted + u)
    lifted = lifted + 8

    def first_end(r, act):
        delta = mm(proj[...], act)
        updated = state[r] + delta[:64]
        heads[r] = delta[64:65, :] + delta[65:66, :]
        halves = [updated[:, s * 128 : (s + 1) * 128] for s in range(2)]
        put(x2, r - DMAX, [norm(a, cols[3], r) for a in halves], d2)

    def second_end(r, act):
        y = mm(last[...], act)
        y = y[0:1, :] + y[1:2, :] + heads[r + HALO]
        for s in range(2):
            out[s, pl.ds(r, 1), :] += y[:, s * 128 : (s + 1) * 128]

    def first_block(r, count):
        for u in range(count):
            act = gelu_of_half(sums1[u % RING][...])
            sums1[u % RING][...] = conv(0, x1, r + RING + u, d1)
            first_end(r + u, act)

    def second_block(r, count, lift_from=None):
        for u in range(count):
            act = gelu_of_half(sums2[u % RING][...])
            sums2[u % RING][...] = conv(1, x2, DMAX + r + RING + u, d2)
            second_end(r + u, act)
            if lift_from is not None and u < LIFTS:
                lift_row(lift_from + u)

    def alone(q, carry):
        first_block(start + q * EARLY, EARLY)
        for u in range(EARLY):
            lift_row(lifted + q * EARLY + u)
        return carry

    lax.fori_loop(0, early, alone, 0)
    for u in range(RING):
        sums2[u][...] = conv(1, x2, DMAX + u, d2)

    def joint(q, carry):
        second_block(q * JOINT, JOINT, lifted + early * EARLY + q * LIFTS)
        first_block(HALO + lead + q * JOINT, JOINT)
        return carry

    trips = (steps - RING - JOINT) // JOINT
    lax.fori_loop(0, trips, joint, 0)
    second_block(trips * JOINT, JOINT)
    for u in range(RING):
        second_end(steps - RING + u, gelu_of_half(sums2[u][...]))


def denoise(spans, dil, *args):
    steps = args[0].shape[1] - 2 * HALO
    hbm = pl.BlockSpec(memory_space=pltpu.HBM)
    return pl.pallas_call(
        lambda *refs: denoise_kernel(spans, *refs),
        out_shape=jax.ShapeDtypeStruct((2, steps, 128), f32),
        in_specs=[hbm] * (1 + len(args)),
        out_specs=pl.BlockSpec(memory_space=pltpu.VMEM),
        scratch_shapes=[pltpu.SMEM((2,), jnp.int32)] + [pltpu.VMEM(a.shape, a.dtype) for a in args] + [
            pltpu.SemaphoreType.DMA((9,)),
            pltpu.VMEM((160, 192, 256), bf16),
            pltpu.VMEM((112, 192, 256), bf16),
            pltpu.VMEM((160, 64, 256), f32),
            pltpu.VMEM((128, 1, 256), f32),
        ] + [pltpu.VMEM((256, 256), f32)] * (2 * RING),
        compiler_params=pltpu.CompilerParams(vmem_limit_bytes=58 * 2**20),
        name="denoise",
    )(dil, *args)


def solution(mesh):
    shots, spans = mesh.shape["shot"], mesh.shape["tm"]

    def per_device(
        noisy_gather, observed, missing, noise_level, dilations, lift_weight, level_weight,
        norm_gain, conv_weight, out_weight, head_weight,
    ):
        masked, noisy, shares, cols, shot_base, wt, proj, last = exchange_inputs(
            shots, spans, jnp.swapaxes(observed, 1, 2), noisy_gather, missing, noise_level[None, :],
            lift_weight, level_weight[None, :], norm_gain, conv_weight, jnp.swapaxes(out_weight, 1, 2), head_weight[None, :],
        )
        return denoise(spans, dilations, noisy, masked, shares, cols, shot_base, wt, proj, last)

    return jax.shard_map(
        per_device,
        mesh=mesh,
        in_specs=(
            P("shot", "tm", None), P(None, "tm", "shot"), P("shot", None), P("shot"),
            P(), P(), P(), P(), P(), P(), P(),
        ),
        out_specs=P("shot", "tm", None),
        check_vma=False,
    )
```
